512 devices in a mesh: req: 8 (over z), head: 8 (over y_lo, core), ffn: 8 (over y_hi, x).
Axes of the slice: x: 4, y: 8 (y_hi: 2, y_lo: 4; y = y_hi * 4 + y_lo), z: 8, core: 2. Of those that a mesh axis runs over, the one named last changes fastest.
Arguments:
- queries: bfloat16 [512, 16384], P(('req', 'ffn'), 'head'), may hold values from -11 to 11
- key_cache: bfloat16 [512, 256, 1024], P(('req', 'ffn'), None, 'head'), may hold values from -4 to 4
- value_cache: bfloat16 [512, 256, 1024], P(('req', 'ffn'), None, 'head'), may hold values from -5 to 5
- new_key: bfloat16 [512, 1024], P(('req', 'ffn'), 'head'), may hold values from -5 to 5
- new_value: bfloat16 [512, 1024], P(('req', 'ffn'), 'head'), may hold values from -5 to 5
- lengths: int32 [512], P(('req', 'ffn')), may hold values from 2 to 256, as said below
- residual: bfloat16 [512, 16384], P(('req', 'ffn'), 'head'), may hold values from -40 to 40
- norm_gain: bfloat16 [16384], P('head'), may hold values from 0.099609375 to 1.8984375
- w_gate: bfloat16 [16384, 32768], P('head', ('req', 'ffn')), may hold values from -0.046875 to 0.046875
- w_down: bfloat16 [32768, 16384], P(('req', 'ffn'), 'head'), may hold values from -0.03125 to 0.03125
Outputs:
- result: bfloat16 [512, 16384], P(('req', 'ffn'), 'head')
The draws below stay inside these ranges and needn't reach their ends.
Inputs may be any that keep to these rules, and one draw needn't show every extreme that they name: `lengths`: every request has at least two cached tokens; some request fills all 256 slots.
All inputs are finite; a program needn't handle non-finite values.
Results may differ from the reference program's by a relative error of at most 0.0075.
Values may be sent and summed in bfloat16 or wider, within the bound.
A program may use at most 64 MiB of HBM per device.

```python
import jax
import jax.numpy as jnp
from jax import lax

D = 16384
QH = 128
KVH = 8
HD = 128
FF = 32768
CACHE = 256
ROWS = 512


def draw_queries(key, part):
    key = jax.random.fold_in(key, 3)
    base_draw = jnp.clip(jax.random.normal(key, (ROWS, QH * HD), jnp.float32), -6.0, 6.0)
    return base_draw.astype(jnp.bfloat16)


def draw_key_cache(key, part):
    key = jax.random.fold_in(key, 4)
    base_draw = jnp.clip(jax.random.normal(key, (ROWS, CACHE, KVH * HD), jnp.float32), -4.0, 4.0)
    return base_draw.astype(jnp.bfloat16)


def draw_lengths(key, part):
    key = jax.random.fold_in(key, 5)
    first_key, second_key = jax.random.split(key)
    drawn = jax.random.randint(first_key, (ROWS,), 2, CACHE + 1)
    chosen = jax.random.randint(second_key, (), 0, ROWS)
    return jnp.where(jnp.arange(ROWS) == chosen, CACHE, drawn).astype(jnp.int32)


def draw_residual(key, part):
    key = jax.random.fold_in(key, 7)
    first_key, second_key = jax.random.split(key)
    row_scale = 10.0 ** jax.random.uniform(first_key, (ROWS, 1), jnp.float32)
    column_scale = 10.0 ** (jnp.arange(D, dtype=jnp.float32) / D)[None, :]
    noise = jnp.clip(jax.random.normal(second_key, (ROWS, D), jnp.float32), -4.0, 4.0)
    return (0.1 * noise * row_scale * column_scale).astype(jnp.bfloat16)


def level_of(rng, shape, shards, smallest, top_value):
    gain, own = 1.0, jax.random.fold_in(rng, 6)
    for dim, blocks in shards:
        steps = jnp.exp(jax.random.uniform(jax.random.fold_in(own, dim), (blocks,), jnp.float32, smallest / len(shards), top_value / len(shards)))
        gain = gain * jnp.repeat(steps, shape[dim] // blocks).reshape([-1 if axis == dim else 1 for axis in range(len(shape))])
    return gain


def normal_values(rng, shape, deviation, reach, cuts=(), kind=jnp.bfloat16):
    values = deviation * jax.random.normal(rng, shape, jnp.float32)
    if cuts:
        values = values * level_of(rng, shape, cuts, -0.22, 0.18)
    return jnp.clip(values, -reach, reach).astype(kind)


def setup_inputs(seed: int = 0) -> dict:
    splits = jax.random.split(jax.random.key(seed), 11)
    queries = draw_queries(jax.random.fold_in(splits[10], 71), 0)
    key_cache = draw_key_cache(jax.random.fold_in(splits[10], 71), 0)
    value_cache = normal_values(splits[2], (ROWS, CACHE, KVH * HD), 1.0, 5.0, ((0, 64), (2, 8)))
    new_key = normal_values(splits[3], (ROWS, KVH * HD), 1.0, 5.0, ((0, 64), (1, 8)))
    new_value = normal_values(splits[4], (ROWS, KVH * HD), 1.0, 5.0, ((0, 64), (1, 8)))
    lengths = draw_lengths(jax.random.fold_in(splits[10], 71), 0)
    residual = draw_residual(jax.random.fold_in(splits[10], 71), 0)
    norm_gain = jnp.clip(1.0 + 0.18 * jax.random.normal(splits[7], (D,), jnp.float32), 0.099609375, 1.8984375).astype(jnp.bfloat16)
    w_gate = normal_values(splits[8], (D, FF), D ** -0.5, 0.046875, ((0, 8), (1, 64)))
    w_down = normal_values(splits[9], (FF, D), FF ** -0.5, 0.03125, ((0, 64), (1, 8)))
    return dict(queries=queries, key_cache=key_cache, value_cache=value_cache, new_key=new_key, new_value=new_value, lengths=lengths, residual=residual, norm_gain=norm_gain, w_gate=w_gate, w_down=w_down)


EPSILON = 1e-05

def attend(queries, key_cache, value_cache, new_key, new_value, lengths):
    row_count = queries.shape[0]
    per_group = QH // KVH
    score_scale = HD ** (-0.5)
    query_heads = queries.astype(jnp.float32).reshape(row_count, KVH, per_group, HD)
    key_block = key_cache.astype(jnp.float32).reshape(row_count, CACHE, KVH, HD)
    value_block = value_cache.astype(jnp.float32).reshape(row_count, CACHE, KVH, HD)
    fresh_key = new_key.astype(jnp.float32).reshape(row_count, KVH, HD)
    fresh_value = new_value.astype(jnp.float32).reshape(row_count, KVH, HD)
    scores = jnp.einsum('rkgd,rlkd->rkgl', query_heads, key_block) * score_scale
    self_score = jnp.einsum('rkgd,rkd->rkg', query_heads, fresh_key) * score_scale
    visible = jnp.arange(CACHE, dtype=jnp.int32)[None, None, None, :] < lengths.astype(jnp.int32)[:, None, None, None]
    maximum = jnp.maximum(lax.optimization_barrier(jnp.max(jnp.where(visible, scores, -1e+30), axis=-1)), self_score)
    raised = jnp.where(visible, jnp.exp(scores - maximum[..., None]), 0.0)
    self_raised = jnp.exp(self_score - maximum)
    totals = lax.optimization_barrier(jnp.sum(raised, axis=-1)) + self_raised
    weights = (raised / totals[..., None]).astype(jnp.bfloat16)
    self_weight = (self_raised / totals).astype(jnp.bfloat16)
    blended = jnp.einsum('rkgl,rlkd->rkgd', weights.astype(jnp.float32), value_block)
    blended = blended + self_weight.astype(jnp.float32)[..., None] * fresh_value[:, :, None, :]
    return blended.reshape(row_count, KVH * per_group * HD).astype(jnp.bfloat16)

def reference(queries, key_cache, value_cache, new_key, new_value, lengths, residual, norm_gain, w_gate, w_down):
    attended = attend(queries, key_cache, value_cache, new_key, new_value, lengths)
    stream = (residual.astype(jnp.float32) + attended.astype(jnp.float32)).astype(jnp.bfloat16)
    stream_wide = stream.astype(jnp.float32)
    squares = lax.optimization_barrier(jnp.sum(stream_wide * stream_wide, axis=1))
    inverse = lax.rsqrt(squares / D + EPSILON)
    normed = (stream_wide * inverse[:, None] * norm_gain.astype(jnp.float32)[None, :]).astype(jnp.bfloat16)
    gate_pre = jnp.dot(normed, w_gate, preferred_element_type=jnp.float32)
    hidden = jax.nn.silu(gate_pre).astype(jnp.bfloat16)
    ffn_out = jnp.dot(hidden, w_down, preferred_element_type=jnp.float32)
    return (stream_wide + ffn_out).astype(jnp.bfloat16)
```

```python
import jax
import jax.numpy as jnp
from jax import lax
from jax.experimental import pallas as pl
from jax.experimental.pallas import tpu as pltpu
from jax.sharding import PartitionSpec as P

D = 16384
EPSILON = 1e-05
NZ = 8
NX = 4
NY = 4
ROWS = 8
HEADS = 16
HD = 128
CACHE = 256
WIDTH = 2048
HALF = WIDTH // 2
HIDDEN = 512
QUARTER = HIDDEN // NY
MESH = pl.DeviceIdType.MESH
F32 = jnp.float32
BF16 = jnp.bfloat16

GROUPS = (
    (("E", 0), ("O", 0)),
    (("E", 1), ("E", 7)),
    (("E", 2), ("E", 6), ("O", 1), ("O", 3)),
    (("E", 3), ("E", 5)),
    (("E", 4), ("O", 2)),
)
FLOW = {"E": 0, "O": 1}
BLOCKS = {"E": NX, "O": NZ}


def group_rows(group):
    return sum(BLOCKS[kind] * ROWS for kind, _ in group)


def offset_of(g):
    return sum(group_rows(group) for group in GROUPS[:g]) // 2


RING_ORDER = (("p", 0), ("m", 1), ("p", 1), ("m", 0))


def hops_of(n, direction, half):
    far = 0 if direction == "p" else 1
    return n // 2 if half == far else n // 2 - 1


def fold(wide):
    return jnp.concatenate([wide[:, :HALF], wide[:, HALF:]], axis=0)


def unfold(folded):
    return jnp.concatenate([folded[:ROWS], folded[ROWS:]], axis=1)


def kernel(
    q_ref,
    k_hbm,
    v_hbm,
    nk_ref,
    nv_ref,
    len_ref,
    res_ref,
    gain_ref,
    wg_hbm,
    wd_hbm,
    out_ref,
    k_ref,
    v_ref,
    wg_ref,
    wd_ref,
    sq_ref,
    ysend,
    yrecv,
    stream_ref,
    x_ref,
    xu_ref,
    p_ref,
    s1_send,
    s1_recv,
    s2_own,
    s2_send,
    s2_recv,
    hid_ref,
    d_ref,
    re_ref,
    ro_ref,
    fe_ref,
    fo_ref,
    fsum_ref,
    zsend,
    zrecv,
    load_sem,
    send_sem,
    recv_sem,
):
    z = lax.axis_index("req")
    head = lax.axis_index("head")
    ffn = lax.axis_index("ffn")
    yq, core = head // 2, head % 2
    yh, x = ffn // NX, ffn % NX

    def along_z(step):
        return {"req": (z + step) % NZ}

    def along_x(step):
        return {"ffn": yh * NX + (x + step) % NX}

    def along_y(step):
        return {"head": ((yq + step) % NY) * 2 + core}

    other_core = {"head": yq * 2 + 1 - core}
    other_half = {"ffn": (1 - yh) * NX + x}

    def same_rows(dh, dk):
        return {"ffn": ((yh + dh) % 2) * NX + x, "head": (head + dk) % 8}

    loads = []
    for i, (src, dst) in enumerate(
        ((k_hbm, k_ref), (v_hbm, v_ref), (wg_hbm, wg_ref), (wd_hbm, wd_ref))
    ):
        copy = pltpu.make_async_copy(src, dst, load_sem.at[i])
        copy.start()
        loads.append(copy)

    peers = [same_rows(dh, dk) for dh in range(2) for dk in range(8) if dh or dk]
    peers += [along_x(k) for k in range(1, NX)]
    peers += [along_z(k) for k in range(1, NZ)]
    barrier = pltpu.get_barrier_semaphore()
    for peer in peers:
        pl.semaphore_signal(barrier, inc=1, device_id=peer, device_id_type=MESH)

    copies = []

    def send(src, dst, device):
        i = len(copies)
        copy = pltpu.make_async_remote_copy(
            src_ref=src,
            dst_ref=dst,
            send_sem=send_sem.at[i],
            recv_sem=recv_sem.at[i],
            device_id=device,
            device_id_type=MESH,
        )
        copy.start()
        copies.append(copy)
        return copy

    q = q_ref[...].astype(F32)
    q_all = jnp.concatenate([q[:, HD * j : HD * (j + 1)] for j in range(HEADS)], axis=0)
    request = lax.broadcasted_iota(jnp.int32, (HEADS * ROWS, 1), 0) % ROWS
    limit = jnp.zeros((HEADS * ROWS, 1), jnp.int32)
    for r in range(ROWS):
        limit = jnp.where(request == r, len_ref[r], limit)
    scale = HD ** (-0.5)
    new_key = jnp.concatenate([nk_ref[...].astype(F32)] * HEADS, axis=0)
    new_value = jnp.concatenate([nv_ref[...].astype(F32)] * HEADS, axis=0)
    self_score = jnp.sum(q_all * new_key, axis=1, keepdims=True) * scale
    loads[0].wait()
    scores = jnp.zeros((HEADS * ROWS, CACHE), F32)
    for r in range(ROWS):
        scores += lax.dot_general(
            jnp.where(request == r, q_all, 0.0).astype(BF16),
            k_ref[r],
            (((1,), (1,)), ((), ())),
            preferred_element_type=F32,
        )
    scores = scores * scale
    visible = lax.broadcasted_iota(jnp.int32, scores.shape, 1) < limit
    maximum = jnp.maximum(
        jnp.max(jnp.where(visible, scores, -1e30), axis=1, keepdims=True), self_score
    )
    raised = jnp.where(visible, jnp.exp(scores - maximum), 0.0)
    self_raised = jnp.exp(self_score - maximum)
    totals = jnp.sum(raised, axis=1, keepdims=True) + self_raised
    weights = raised / totals
    self_weight = (self_raised / totals).astype(BF16).astype(F32)
    loads[1].wait()
    blended = self_weight * new_value
    for r in range(ROWS):
        blended += jnp.dot(
            jnp.where(request == r, weights, 0.0).astype(BF16),
            v_ref[r],
            preferred_element_type=F32,
        )
    attended = jnp.concatenate(
        [blended[ROWS * j : ROWS * (j + 1)] for j in range(HEADS)], axis=1
    ).astype(BF16)
    stream = (res_ref[...].astype(F32) + attended.astype(F32)).astype(BF16).astype(F32)
    stream_ref[...] = stream
    squares = stream * stream
    part = squares[:, :HD]
    for j in range(1, HEADS):
        part += squares[:, HD * j : HD * (j + 1)]
    sq_ref[0, 0] = part
    ysend[...] = fold(stream).astype(BF16)

    pl.semaphore_wait(barrier, len(peers))

    ycopy = send(ysend, yrecv, other_half)
    sq_copies = []
    for dh in range(2):
        for dk in range(8):
            if dh or dk:
                sq_copies.append(
                    send(sq_ref.at[0, 0], sq_ref.at[dh, (8 - dk) % 8], same_rows(dh, dk))
                )
    gain = gain_ref[...].astype(F32)

    def normed(rows, dh):
        total = sq_ref[dh, 0]
        for dk in range(1, 8):
            total += sq_ref[dh, dk]
        inverse = lax.rsqrt(jnp.sum(total, axis=1, keepdims=True) / D + EPSILON)
        return fold(rows * inverse * gain).astype(BF16)

    for copy in sq_copies:
        copy.wait_recv()
    x_ref[yh, 0] = normed(stream, 0)
    ycopy.wait_recv()
    x_ref[1 - yh, 0] = normed(unfold(yrecv[...].astype(F32)), 1)

    o_first = []
    for k in (4, 3, 5, 2, 6, 1, 7):
        o_first.append(send(x_ref.at[1, 0], x_ref.at[1, NZ - k], along_z(k)))
    e_first = []
    for k in (2, 1, 3):
        e_first.append(send(x_ref.at[0, 0], x_ref.at[0, NX - k], along_x(k)))

    rings = {"E": (NZ, along_z), "O": (NX, along_x)}

    def chunk(ref, kind, slot, half):
        blocks = BLOCKS[kind] // 2
        return ref.at[FLOW[kind], pl.ds(slot * BLOCKS[kind] + half * blocks, blocks)]

    arriving = {}

    def gather_hop(kind, s):
        n, along = rings[kind]
        for direction, half in RING_ORDER:
            if (kind, direction, half, s - 1) in arriving:
                arriving[kind, direction, half, s - 1].wait_recv()
            if s >= hops_of(n, direction, half):
                continue
            step = 1 if direction == "p" else -1
            arriving[kind, direction, half, s] = send(
                chunk(x_ref, kind, (-step * s) % n, half),
                chunk(x_ref, kind, (-step * (s + 1)) % n, half),
                along(step),
            )

    step_copies = {}

    def gate(g):
        row = 0
        for kind, slot in GROUPS[g]:
            n = BLOCKS[kind]
            folded = x_ref[FLOW[kind], slot * n : (slot + 1) * n].astype(F32)
            low = folded[:, :ROWS].reshape(n * ROWS, HALF).astype(BF16)
            high = folded[:, ROWS:].reshape(n * ROWS, HALF).astype(BF16)
            xu_ref[row : row + n * ROWS, :HALF] = low
            xu_ref[row : row + n * ROWS, HALF:] = high
            row += n * ROWS
        m, o = row // 2, offset_of(g)
        value = jnp.dot(xu_ref[:row, :], wg_ref[...], preferred_element_type=F32)
        p_ref[0, o : o + m] = value[:m]
        p_ref[1, o : o + m] = value[m:]
        s1_send[o : o + m] = p_ref[1 - core, o : o + m].astype(BF16)
        step_copies[1, g] = [
            send(s1_send.at[pl.ds(o, m)], s1_recv.at[pl.ds(o, m)], other_core)
        ]

    def reduce_y(g):
        m, o = group_rows(GROUPS[g]) // 2, offset_of(g)
        for copy in step_copies[1, g]:
            copy.wait_recv()
        value = p_ref[core, o : o + m] + s1_recv[o : o + m].astype(F32)
        for j in range(NY):
            piece = value[:, QUARTER * j : QUARTER * (j + 1)]
            s2_own[j, o : o + m] = piece
            s2_send[j, o : o + m] = piece.astype(BF16)
        step_copies[2, g] = [
            send(
                s2_send.at[(yq + k) % NY, pl.ds(o, m)],
                s2_recv.at[k - 1, pl.ds(o, m)],
                along_y(k),
            )
            for k in (2, 1, 3)
        ]

    def activate(g):
        m, o = group_rows(GROUPS[g]) // 2, offset_of(g)
        for copy in step_copies[2, g]:
            copy.wait_recv()
        value = s2_own[yq, o : o + m]
        for k in range(NY - 1):
            value += s2_recv[k, o : o + m].astype(F32)
        hid_ref[core, yq, o : o + m] = (value / (1.0 + jnp.exp(-value))).astype(BF16)
        piece = hid_ref.at[core, yq, pl.ds(o, m)]
        step_copies[3, g] = [send(piece, piece, along_y(k)) for k in (2, 1, 3)]

    def share_core(g):
        m, o = group_rows(GROUPS[g]) // 2, offset_of(g)
        for copy in step_copies[3, g]:
            copy.wait_recv()
        piece = hid_ref.at[core, :, pl.ds(o, m)]
        step_copies[4, g] = [send(piece, piece, other_core)]

    def down(g):
        m, o = group_rows(GROUPS[g]) // 2, offset_of(g)
        for copy in step_copies[4, g]:
            copy.wait_recv()
        hidden = jnp.concatenate(
            [
                jnp.concatenate([hid_ref[c, j, o : o + m] for j in range(NY)], axis=1)
                for c in range(2)
            ],
            axis=0,
        )
        tile = 256
        for t in range(HALF // tile):
            columns = pl.ds(t * tile, tile)
            low = jnp.dot(
                hidden, wd_ref[:, t * tile : (t + 1) * tile], preferred_element_type=F32
            ).reshape(2 * m // ROWS, ROWS, tile)
            high = jnp.dot(
                hidden,
                wd_ref[:, HALF + t * tile : HALF + (t + 1) * tile],
                preferred_element_type=F32,
            ).reshape(2 * m // ROWS, ROWS, tile)
            both = jnp.concatenate([low, high], axis=1).astype(BF16)
            row = 0
            for kind, slot in GROUPS[g]:
                n = BLOCKS[kind]
                d_ref[FLOW[kind], slot * n : (slot + 1) * n, :, columns] = both[row : row + n]
                row += n

    for copy in e_first:
        copy.wait_recv()
    gather_hop("E", 0)
    for copy in o_first:
        copy.wait_recv()
    gather_hop("O", 0)
    loads[2].wait()
    gate(0)
    gather_hop("E", 1)
    gate(1)
    reduce_y(0)
    gather_hop("O", 1)
    gather_hop("E", 2)
    activate(0)
    gate(2)
    reduce_y(1)
    gather_hop("E", 3)
    activate(1)
    share_core(0)
    gate(3)
    reduce_y(2)
    activate(2)
    share_core(1)
    gather_hop("E", 4)
    gather_hop("O", 2)
    gate(4)
    reduce_y(3)
    loads[3].wait()
    down(0)
    reduce_y(4)
    activate(3)
    share_core(2)
    down(1)
    activate(4)
    share_core(3)
    down(2)
    share_core(4)
    down(3)
    down(4)

    recv_at = {"E": {}, "O": {}}
    for kind in ("E", "O"):
        n, _ = rings[kind]
        count = 0
        for direction, half in RING_ORDER:
            for s in range(hops_of(n, direction, half)):
                recv_at[kind][direction, half, s] = count
                count += 1
    recv_refs = {"E": re_ref, "O": ro_ref}
    sums = {}

    def scatter_hop(kind, s):
        n, along = rings[kind]
        landing = recv_refs[kind]
        blocks = BLOCKS[kind] // 2
        for direction, half in RING_ORDER:
            hops, t = hops_of(n, direction, half), s
            if t >= hops:
                continue
            step = 1 if direction == "p" else -1
            slot = (step * (hops - t)) % n
            if t > 0:
                sums[kind, direction, half, t - 1].wait_recv()
                first = slot * BLOCKS[kind] + half * blocks
                own = d_ref[FLOW[kind], first : first + blocks].astype(F32)
                came = landing[recv_at[kind][direction, half, t - 1]].astype(F32)
                d_ref[FLOW[kind], first : first + blocks] = (own + came).astype(BF16)
            sums[kind, direction, half, t] = send(
                chunk(d_ref, kind, slot, half),
                landing.at[recv_at[kind][direction, half, t]],
                along(step),
            )

    def scatter_end(kind):
        n, _ = rings[kind]
        blocks = BLOCKS[kind] // 2
        for half in range(2):
            value = d_ref[FLOW[kind], half * blocks : (half + 1) * blocks].astype(F32)
            for direction in ("p", "m"):
                last = hops_of(n, direction, half) - 1
                sums[kind, direction, half, last].wait_recv()
                value += recv_refs[kind][recv_at[kind][direction, half, last]].astype(F32)
            d_ref[FLOW[kind], half * blocks : (half + 1) * blocks] = value.astype(BF16)

    scatter_hop("E", 0)
    scatter_hop("O", 0)
    scatter_hop("E", 1)
    scatter_hop("O", 1)
    scatter_hop("E", 2)
    scatter_end("O")
    o_last = []
    for k in (4, 3, 5, 2, 6, 1, 7):
        o_last.append(send(d_ref.at[1, k], fo_ref.at[k - 1], along_z(k)))
    scatter_hop("E", 3)
    scatter_end("E")
    e_last = []
    for k in (2, 1, 3):
        e_last.append(send(d_ref.at[0, k], fe_ref.at[k - 1], along_x(k)))
    for which, (lasts, landing) in enumerate(((e_last, fe_ref), (o_last, fo_ref))):
        value = d_ref[which, 0].astype(F32)
        for copy in lasts:
            copy.wait_recv()
        for k in range(len(lasts)):
            value += landing[k].astype(F32)
        fsum_ref[which] = value
    zsend[...] = fsum_ref[1 - yh].astype(BF16)
    zcopy = send(zsend, zrecv, other_half)
    zcopy.wait_recv()
    total = fsum_ref[yh] + zrecv[...].astype(F32)
    out_ref[...] = (stream_ref[...] + unfold(total)).astype(BF16)

    for copy in copies:
        copy.wait_send()


COPIES = 1 + 15 + 7 + 3 + 14 + 6 + 8 * len(GROUPS) + 14 + 6 + 7 + 3 + 1


def per_device(
    queries,
    key_cache,
    value_cache,
    new_key,
    new_value,
    lengths,
    residual,
    norm_gain,
    w_gate,
    w_down,
):
    vmem = pl.BlockSpec(memory_space=pltpu.VMEM)
    smem = pl.BlockSpec(memory_space=pltpu.SMEM)
    hbm = pl.BlockSpec(memory_space=pl.ANY)
    block = (2 * ROWS, HALF)
    most = max(group_rows(group) for group in GROUPS)
    return pl.pallas_call(
        kernel,
        out_shape=jax.ShapeDtypeStruct((ROWS, WIDTH), BF16),
        in_specs=[vmem, hbm, hbm, vmem, vmem, smem, vmem, vmem, hbm, hbm],
        out_specs=vmem,
        scratch_shapes=[
            pltpu.VMEM((ROWS, CACHE, HD), BF16),
            pltpu.VMEM((ROWS, CACHE, HD), BF16),
            pltpu.VMEM((WIDTH, HIDDEN), BF16),
            pltpu.VMEM((HIDDEN, WIDTH), BF16),
            pltpu.VMEM((2, 8, ROWS, HD), F32),
            pltpu.VMEM(block, BF16),
            pltpu.VMEM(block, BF16),
            pltpu.VMEM((ROWS, WIDTH), F32),
            pltpu.VMEM((2, NZ * NX) + block, BF16),
            pltpu.VMEM((most, WIDTH), BF16),
            pltpu.VMEM((2, 256, HIDDEN), F32),
            pltpu.VMEM((256, HIDDEN), BF16),
            pltpu.VMEM((256, HIDDEN), BF16),
            pltpu.VMEM((NY, 256, QUARTER), F32),
            pltpu.VMEM((NY, 256, QUARTER), BF16),
            pltpu.VMEM((NY - 1, 256, QUARTER), BF16),
            pltpu.VMEM((2, NY, 256, QUARTER), BF16),
            pltpu.VMEM((2, NZ * NX) + block, BF16),
            pltpu.VMEM((14, NX // 2) + block, BF16),
            pltpu.VMEM((6, NZ // 2) + block, BF16),
            pltpu.VMEM((NX - 1,) + block, BF16),
            pltpu.VMEM((NZ - 1,) + block, BF16),
            pltpu.VMEM((2,) + block, F32),
            pltpu.VMEM(block, BF16),
            pltpu.VMEM(block, BF16),
            pltpu.SemaphoreType.DMA((4,)),
            pltpu.SemaphoreType.DMA((COPIES,)),
            pltpu.SemaphoreType.DMA((COPIES,)),
        ],
        compiler_params=pltpu.CompilerParams(
            collective_id=0, has_side_effects=True, vmem_limit_bytes=60 * 1024 * 1024
        ),
        cost_estimate=pl.CostEstimate(
            flops=2 * 2 * 512 * WIDTH * HIDDEN, bytes_accessed=6 * 2**20, transcendentals=0
        ),
    )(
        queries,
        key_cache,
        value_cache,
        new_key,
        new_value,
        lengths,
        residual,
        norm_gain.reshape(1, WIDTH),
        w_gate,
        w_down,
    )


def solution(mesh):
    rows = ("req", "ffn")
    return jax.shard_map(
        per_device,
        mesh=mesh,
        in_specs=(
            P(rows, "head"),
            P(rows, None, "head"),
            P(rows, None, "head"),
            P(rows, "head"),
            P(rows, "head"),
            P(rows),
            P(rows, "head"),
            P("head"),
            P("head", rows),
            P(rows, "head"),
        ),
        out_specs=P(rows, "head"),
        check_vma=False,
    )
```

```python
import jax
import jax.numpy as jnp
from jax import lax
from jax.experimental import pallas as pl
from jax.experimental.pallas import tpu as pltpu
from jax.sharding import PartitionSpec as P

D = 16384
EPSILON = 1e-05
NZ = 8
NX = 4
NY = 4
ROWS = 8
HEADS = 16
HD = 128
CACHE = 256
WIDTH = 2048
HALF = WIDTH // 2
HIDDEN = 512
QUARTER = HIDDEN // NY
MESH = pl.DeviceIdType.MESH
F32 = jnp.float32
BF16 = jnp.bfloat16

GROUPS = (
    (("E", 0), ("O", 0)),
    (("E", 1), ("E", 7)),
    (("E", 2), ("E", 6), ("O", 1), ("O", 3)),
    (("E", 3), ("E", 5)),
    (("E", 4), ("O", 2)),
)
FLOW = {"E": 0, "O": 1}
BLOCKS = {"E": NX, "O": NZ}
Z_ORDER = (0, 4, 3, 5, 2, 6, 1, 7)


def group_rows(group):
    return sum(BLOCKS[kind] * ROWS for kind, _ in group)


def offset_of(g):
    return sum(group_rows(group) for group in GROUPS[:g]) // 2


FAR = (("p", 0), ("m", 1))
NEAR = (("p", 1), ("m", 0))
RING_ORDER = FAR + NEAR


def hops_of(n, direction, half):
    return n // 2 if (direction, half) in FAR else n // 2 - 1


def fold(wide):
    return jnp.concatenate([wide[:, :HALF], wide[:, HALF:]], axis=0)


def unfold(folded):
    return jnp.concatenate([folded[:ROWS], folded[ROWS:]], axis=1)


def kernel(
    q_ref,
    k_hbm,
    v_hbm,
    nk_ref,
    nv_ref,
    len_ref,
    res_ref,
    gain_ref,
    wg_hbm,
    wd_hbm,
    out_ref,
    k_ref,
    v_ref,
    wg_ref,
    wd_ref,
    sq_ref,
    ysend,
    yrecv,
    stream_ref,
    x_ref,
    xu_ref,
    p_ref,
    s1_send,
    s1_recv,
    s2_own,
    s2_send,
    s2_recv,
    hid_ref,
    d_ref,
    re_ref,
    ro_ref,
    fe_ref,
    fo_ref,
    zsend,
    zrecv,
    load_sem,
    send_sem,
    recv_sem,
):
    z = lax.axis_index("req")
    head = lax.axis_index("head")
    ffn = lax.axis_index("ffn")
    yq, core = head // 2, head % 2
    yh, x = ffn // NX, ffn % NX

    def along_z(step):
        return {"req": (z + step) % NZ}

    def along_x(step):
        return {"ffn": yh * NX + (x + step) % NX}

    def along_y(step):
        return {"head": ((yq + step) % NY) * 2 + core}

    other_core = {"head": yq * 2 + 1 - core}
    other_half = {"ffn": (1 - yh) * NX + x}

    def same_rows(dh, dk):
        return {"ffn": ((yh + dh) % 2) * NX + x, "head": (head + dk) % 8}

    loads = []
    for i, (src, dst) in enumerate(
        ((k_hbm, k_ref), (v_hbm, v_ref), (wg_hbm, wg_ref), (wd_hbm, wd_ref))
    ):
        copy = pltpu.make_async_copy(src, dst, load_sem.at[i])
        copy.start()
        loads.append(copy)

    peers = [same_rows(dh, dk) for dh in range(2) for dk in range(8) if dh or dk]
    peers += [along_x(k) for k in range(1, NX)]
    peers += [along_z(k) for k in range(1, NZ)]
    barrier = pltpu.get_barrier_semaphore()
    for peer in peers:
        pl.semaphore_signal(barrier, inc=1, device_id=peer, device_id_type=MESH)

    copies = []

    def send(src, dst, device):
        i = len(copies)
        copy = pltpu.make_async_remote_copy(
            src_ref=src,
            dst_ref=dst,
            send_sem=send_sem.at[i],
            recv_sem=recv_sem.at[i],
            device_id=device,
            device_id_type=MESH,
        )
        copy.start()
        copies.append(copy)
        return copy

    q = q_ref[...].astype(F32)
    q_all = jnp.concatenate([q[:, HD * j : HD * (j + 1)] for j in range(HEADS)], axis=0)
    request = lax.broadcasted_iota(jnp.int32, (HEADS * ROWS, 1), 0) % ROWS
    limit = jnp.zeros((HEADS * ROWS, 1), jnp.int32)
    for r in range(ROWS):
        limit = jnp.where(request == r, len_ref[r], limit)
    scale = HD ** (-0.5)
    new_key = jnp.concatenate([nk_ref[...].astype(F32)] * HEADS, axis=0)
    new_value = jnp.concatenate([nv_ref[...].astype(F32)] * HEADS, axis=0)
    self_score = jnp.sum(q_all * new_key, axis=1, keepdims=True) * scale
    loads[0].wait()
    scores = jnp.zeros((HEADS * ROWS, CACHE), F32)
    for r in range(ROWS):
        scores += lax.dot_general(
            jnp.where(request == r, q_all, 0.0).astype(BF16),
            k_ref[r],
            (((1,), (1,)), ((), ())),
            preferred_element_type=F32,
        )
    scores = scores * scale
    visible = lax.broadcasted_iota(jnp.int32, scores.shape, 1) < limit
    maximum = jnp.maximum(
        jnp.max(jnp.where(visible, scores, -1e30), axis=1, keepdims=True), self_score
    )
    raised = jnp.where(visible, jnp.exp(scores - maximum), 0.0)
    self_raised = jnp.exp(self_score - maximum)
    totals = jnp.sum(raised, axis=1, keepdims=True) + self_raised
    weights = raised / totals
    self_weight = (self_raised / totals).astype(BF16).astype(F32)
    loads[1].wait()
    blended = self_weight * new_value
    for r in range(ROWS):
        blended += jnp.dot(
            jnp.where(request == r, weights, 0.0).astype(BF16),
            v_ref[r],
            preferred_element_type=F32,
        )
    attended = jnp.concatenate(
        [blended[ROWS * j : ROWS * (j + 1)] for j in range(HEADS)], axis=1
    ).astype(BF16)
    stream = (res_ref[...].astype(F32) + attended.astype(F32)).astype(BF16).astype(F32)
    stream_ref[...] = stream
    squares = stream * stream
    part = squares[:, :HD]
    for j in range(1, HEADS):
        part += squares[:, HD * j : HD * (j + 1)]
    sq_ref[0, 0] = part
    ysend[...] = fold(stream).astype(BF16)

    pl.semaphore_wait(barrier, len(peers))

    def send_squares(dh):
        return [
            send(sq_ref.at[0, 0], sq_ref.at[dh, (8 - dk) % 8], same_rows(dh, dk))
            for dk in range(8)
            if dh or dk
        ]

    sq_own = send_squares(0)
    ycopy = send(ysend, yrecv, other_half)
    sq_other = send_squares(1)
    gain = gain_ref[...].astype(F32).reshape(1, WIDTH)

    def normed(rows, dh):
        total = sq_ref[dh, 0]
        for dk in range(1, 8):
            total += sq_ref[dh, dk]
        inverse = lax.rsqrt(jnp.sum(total, axis=1, keepdims=True) / D + EPSILON)
        return fold(rows * inverse * gain).astype(BF16)

    o_first, e_first = {}, {}

    def first_sends(kind):
        if kind == "O":
            for copy in sq_own:
                copy.wait_recv()
            x_ref[1, 0] = normed(stream_ref[...], 0)
            for slot in range(1, NZ):
                o_first[slot] = send(
                    x_ref.at[1, 0], x_ref.at[1, slot], along_z(-Z_ORDER[slot])
                )
        else:
            for copy in sq_other:
                copy.wait_recv()
            ycopy.wait_recv()
            x_ref[0, 0] = normed(unfold(yrecv[...].astype(F32)), 1)
            for slot in (1, 2, 3):
                e_first[slot] = send(x_ref.at[0, 0], x_ref.at[0, slot], along_x(-slot))

    def first_end(kind, half):
        blocks = BLOCKS[kind] // 2
        for slot in range(half * blocks, (half + 1) * blocks):
            if slot:
                (e_first if kind == "E" else o_first)[slot].wait_recv()

    rings = {"E": (NZ, along_z), "O": (NX, along_x)}

    def chunk(ref, kind, slot, half):
        blocks = BLOCKS[kind] // 2
        return ref.at[FLOW[kind], pl.ds(slot * BLOCKS[kind] + half * blocks, blocks)]

    arriving, skipping = {}, {}

    def gather_end():
        for copy in skipping.values():
            copy.wait_recv()

    def gather_hop(kind, s, which=RING_ORDER):
        n, along = rings[kind]
        for direction, half in which:
            if (kind, direction, half, s - 1) in arriving:
                arriving[kind, direction, half, s - 1].wait_recv()
            step = 1 if direction == "p" else -1
            hops = hops_of(n, direction, half)
            skip = kind == "E" and hops == n // 2
            if s < hops - skip:
                arriving[kind, direction, half, s] = send(
                    chunk(x_ref, kind, (-step * s) % n, half),
                    chunk(x_ref, kind, (-step * (s + 1)) % n, half),
                    along(step),
                )
            if skip and s == hops - 2:
                skipping[direction] = send(
                    chunk(x_ref, kind, (-step * s) % n, half),
                    chunk(x_ref, kind, (-step * (s + 2)) % n, half),
                    along(2 * step),
                )

    step_copies = {}

    def gate(g):
        row = 0
        for kind, slot in GROUPS[g]:
            n = BLOCKS[kind]
            folded = x_ref[FLOW[kind], slot * n : (slot + 1) * n].astype(F32)
            low = folded[:, :ROWS].reshape(n * ROWS, HALF).astype(BF16)
            high = folded[:, ROWS:].reshape(n * ROWS, HALF).astype(BF16)
            xu_ref[row : row + n * ROWS, :HALF] = low
            xu_ref[row : row + n * ROWS, HALF:] = high
            row += n * ROWS
        m, o = row // 2, offset_of(g)
        value = jnp.dot(xu_ref[:row, :], wg_ref[...], preferred_element_type=F32)
        p_ref[0, o : o + m] = value[:m]
        p_ref[1, o : o + m] = value[m:]
        s1_send[o : o + m] = p_ref[1 - core, o : o + m].astype(BF16)
        step_copies[1, g] = [
            send(s1_send.at[pl.ds(o, m)], s1_recv.at[pl.ds(o, m)], other_core)
        ]

    def reduce_y(g):
        m, o = group_rows(GROUPS[g]) // 2, offset_of(g)
        for copy in step_copies[1, g]:
            copy.wait_recv()
        value = p_ref[core, o : o + m] + s1_recv[o : o + m].astype(F32)
        for j in range(NY):
            piece = value[:, QUARTER * j : QUARTER * (j + 1)]
            s2_own[j, o : o + m] = piece
            s2_send[j, o : o + m] = piece.astype(BF16)
        step_copies[2, g] = [
            send(
                s2_send.at[(yq + k) % NY, pl.ds(o, m)],
                s2_recv.at[k - 1, pl.ds(o, m)],
                along_y(k),
            )
            for k in (2, 1, 3)
        ]

    def activate(g):
        m, o = group_rows(GROUPS[g]) // 2, offset_of(g)
        for copy in step_copies[2, g]:
            copy.wait_recv()
        value = s2_own[yq, o : o + m]
        for k in range(NY - 1):
            value += s2_recv[k, o : o + m].astype(F32)
        hid_ref[core, yq, o : o + m] = (value / (1.0 + jnp.exp(-value))).astype(BF16)
        piece = hid_ref.at[core, yq, pl.ds(o, m)]
        step_copies[3, g] = [send(piece, piece, along_y(k)) for k in (2, 1, 3)]

    def share_core(g):
        m, o = group_rows(GROUPS[g]) // 2, offset_of(g)
        for copy in step_copies[3, g]:
            copy.wait_recv()
        piece = hid_ref.at[core, :, pl.ds(o, m)]
        step_copies[4, g] = [send(piece, piece, other_core)]

    def down(g):
        m, o = group_rows(GROUPS[g]) // 2, offset_of(g)
        for copy in step_copies[4, g]:
            copy.wait_recv()
        hidden = jnp.concatenate(
            [
                jnp.concatenate([hid_ref[c, j, o : o + m] for j in range(NY)], axis=1)
                for c in range(2)
            ],
            axis=0,
        )
        tile = 256
        for t in range(HALF // tile):
            columns = pl.ds(t * tile, tile)
            low = jnp.dot(
                hidden, wd_ref[:, t * tile : (t + 1) * tile], preferred_element_type=F32
            ).reshape(2 * m // ROWS, ROWS, tile)
            high = jnp.dot(
                hidden,
                wd_ref[:, HALF + t * tile : HALF + (t + 1) * tile],
                preferred_element_type=F32,
            ).reshape(2 * m // ROWS, ROWS, tile)
            both = jnp.concatenate([low, high], axis=1).astype(BF16)
            row = 0
            for kind, slot in GROUPS[g]:
                n = BLOCKS[kind]
                d_ref[FLOW[kind], slot * n : (slot + 1) * n, :, columns] = both[row : row + n]
                row += n

    recv_at = {"E": {}, "O": {}}
    for kind in ("E", "O"):
        n, _ = rings[kind]
        count = 0
        for direction, half in RING_ORDER:
            for s in range(hops_of(n, direction, half)):
                recv_at[kind][direction, half, s] = count
                count += 1
    recv_refs = {"E": re_ref, "O": ro_ref}
    sums = {}

    def scatter_hop(kind, s, which=RING_ORDER):
        n, along = rings[kind]
        landing = recv_refs[kind]
        blocks = BLOCKS[kind] // 2
        for direction, half in which:
            hops = hops_of(n, direction, half)
            step = 1 if direction == "p" else -1
            slot = (step * (hops - s)) % n
            skip = kind == "E" and hops == n // 2
            came = [s - 1] if s > 0 else []
            if skip:
                came = {0: [], 1: [], 2: [0, 1], 3: [2]}[s]
            first = slot * BLOCKS[kind] + half * blocks
            if came:
                value = d_ref[FLOW[kind], first : first + blocks].astype(F32)
                for t in came:
                    sums[kind, direction, half, t].wait_recv()
                    value += landing[recv_at[kind][direction, half, t]].astype(F32)
                d_ref[FLOW[kind], first : first + blocks] = value.astype(BF16)
            sums[kind, direction, half, s] = send(
                chunk(d_ref, kind, slot, half),
                landing.at[recv_at[kind][direction, half, s]],
                along(2 * step if skip and s == 0 else step),
            )

    def scatter_end(kind, half):
        n, _ = rings[kind]
        blocks = BLOCKS[kind] // 2
        value = d_ref[FLOW[kind], half * blocks : (half + 1) * blocks].astype(F32)
        for direction in ("p", "m"):
            last = hops_of(n, direction, half) - 1
            sums[kind, direction, half, last].wait_recv()
            value += recv_refs[kind][recv_at[kind][direction, half, last]].astype(F32)
        d_ref[FLOW[kind], half * blocks : (half + 1) * blocks] = value.astype(BF16)
        for slot in range(half * blocks, (half + 1) * blocks):
            if slot == 0:
                continue
            if kind == "O":
                last_copies[kind].append(
                    send(d_ref.at[1, slot], fo_ref.at[slot - 1], along_z(Z_ORDER[slot]))
                )
            else:
                last_copies[kind].append(
                    send(d_ref.at[0, slot], fe_ref.at[slot - 1], along_x(slot))
                )

    last_copies = {"E": [], "O": []}

    def last_end(kind):
        landing = fe_ref if kind == "E" else fo_ref
        value = d_ref[FLOW[kind], 0].astype(F32)
        for copy in last_copies[kind]:
            copy.wait_recv()
        for k in range(BLOCKS[kind] - 1):
            value += landing[k].astype(F32)
        return value

    first_sends("O")
    first_sends("E")
    first_end("E", 0)
    gather_hop("E", 0, (("p", 0), ("m", 0)))
    first_end("E", 1)
    gather_hop("E", 0, (("m", 1), ("p", 1)))
    first_end("O", 0)
    gather_hop("O", 0, (("p", 0), ("m", 0)))
    first_end("O", 1)
    gather_hop("O", 0, (("m", 1), ("p", 1)))
    loads[2].wait()
    gather_hop("E", 1)
    gate(0)
    gate(1)
    reduce_y(0)
    reduce_y(1)
    gather_hop("E", 2)
    gather_hop("O", 1)
    gate(2)
    reduce_y(2)
    gather_hop("E", 3)
    gate(3)
    activate(0)
    activate(1)
    reduce_y(3)
    gather_end()
    gather_hop("O", 2)
    gate(4)
    loads[3].wait()
    reduce_y(4)
    activate(2)
    activate(3)
    share_core(0)
    share_core(1)
    down(0)
    down(1)
    activate(4)
    share_core(2)
    down(2)
    share_core(3)
    down(3)
    share_core(4)
    down(4)
    scatter_hop("E", 0, FAR)
    scatter_hop("E", 1, FAR)
    scatter_hop("O", 0, FAR)
    scatter_hop("E", 0, NEAR)
    scatter_hop("O", 0, NEAR)
    scatter_hop("E", 2, FAR)
    scatter_hop("E", 1, NEAR)
    scatter_hop("O", 1, FAR)
    scatter_hop("E", 3, FAR)
    scatter_hop("E", 2, NEAR)
    scatter_end("O", 0)
    scatter_end("O", 1)
    scatter_end("E", 0)
    scatter_end("E", 1)
    zsend[...] = last_end("E").astype(BF16)
    zcopy = send(zsend, zrecv, other_half)
    total = last_end("O")
    zcopy.wait_recv()
    total += zrecv[...].astype(F32)
    out_ref[...] = (stream_ref[...] + unfold(total)).astype(BF16)

    for copy in copies:
        copy.wait_send()


COPIES = 1 + 15 + 7 + 3 + 14 + 6 + 8 * len(GROUPS) + 14 + 6 + 7 + 3 + 1


def per_device(
    queries,
    key_cache,
    value_cache,
    new_key,
    new_value,
    lengths,
    residual,
    norm_gain,
    w_gate,
    w_down,
):
    vmem = pl.BlockSpec(memory_space=pltpu.VMEM)
    smem = pl.BlockSpec(memory_space=pltpu.SMEM)
    hbm = pl.BlockSpec(memory_space=pl.ANY)
    block = (2 * ROWS, HALF)
    most = max(group_rows(group) for group in GROUPS)
    return pl.pallas_call(
        kernel,
        out_shape=jax.ShapeDtypeStruct((ROWS, WIDTH), BF16),
        in_specs=[vmem, hbm, hbm, vmem, vmem, smem, vmem, vmem, hbm, hbm],
        out_specs=vmem,
        scratch_shapes=[
            pltpu.VMEM((ROWS, CACHE, HD), BF16),
            pltpu.VMEM((ROWS, CACHE, HD), BF16),
            pltpu.VMEM((WIDTH, HIDDEN), BF16),
            pltpu.VMEM((HIDDEN, WIDTH), BF16),
            pltpu.VMEM((2, 8, ROWS, HD), F32),
            pltpu.VMEM(block, BF16),
            pltpu.VMEM(block, BF16),
            pltpu.VMEM((ROWS, WIDTH), F32),
            pltpu.VMEM((2, NZ * NX) + block, BF16),
            pltpu.VMEM((most, WIDTH), BF16),
            pltpu.VMEM((2, 256, HIDDEN), F32),
            pltpu.VMEM((256, HIDDEN), BF16),
            pltpu.VMEM((256, HIDDEN), BF16),
            pltpu.VMEM((NY, 256, QUARTER), F32),
            pltpu.VMEM((NY, 256, QUARTER), BF16),
            pltpu.VMEM((NY - 1, 256, QUARTER), BF16),
            pltpu.VMEM((2, NY, 256, QUARTER), BF16),
            pltpu.VMEM((2, NZ * NX) + block, BF16),
            pltpu.VMEM((14, NX // 2) + block, BF16),
            pltpu.VMEM((6, NZ // 2) + block, BF16),
            pltpu.VMEM((NX - 1,) + block, BF16),
            pltpu.VMEM((NZ - 1,) + block, BF16),
            pltpu.VMEM(block, BF16),
            pltpu.VMEM(block, BF16),
            pltpu.SemaphoreType.DMA((4,)),
            pltpu.SemaphoreType.DMA((COPIES,)),
            pltpu.SemaphoreType.DMA((COPIES,)),
        ],
        compiler_params=pltpu.CompilerParams(
            collective_id=0, has_side_effects=True, vmem_limit_bytes=60 * 1024 * 1024
        ),
        cost_estimate=pl.CostEstimate(
            flops=2 * 2 * 512 * WIDTH * HIDDEN, bytes_accessed=6 * 2**20, transcendentals=0
        ),
    )(
        queries,
        key_cache,
        value_cache,
        new_key,
        new_value,
        lengths,
        residual,
        norm_gain,
        w_gate,
        w_down,
    )


def solution(mesh):
    rows = ("req", "ffn")
    return jax.shard_map(
        per_device,
        mesh=mesh,
        in_specs=(
            P(rows, "head"),
            P(rows, None, "head"),
            P(rows, None, "head"),
            P(rows, "head"),
            P(rows, "head"),
            P(rows),
            P(rows, "head"),
            P("head"),
            P("head", rows),
            P(rows, "head"),
        ),
        out_specs=P(rows, "head"),
        check_vma=False,
    )
```

```python
import jax
import jax.numpy as jnp
from jax import lax
from jax.experimental import pallas as pl
from jax.experimental.pallas import tpu as pltpu
from jax.sharding import PartitionSpec as P

D = 16384
EPSILON = 1e-05
NZ = 8
NX = 4
NY = 4
ROWS = 8
HEADS = 16
HD = 128
CACHE = 256
WIDTH = 2048
HALF = WIDTH // 2
HIDDEN = 512
QUARTER = HIDDEN // NY
MESH = pl.DeviceIdType.MESH
F32 = jnp.float32
BF16 = jnp.bfloat16

GROUPS = (
    (("E", 0), ("O", 0)),
    (("E", 1), ("E", 7)),
    (("E", 2), ("E", 6), ("O", 1), ("O", 3)),
    (("E", 3), ("E", 5)),
    (("E", 4), ("O", 2)),
)
FLOW = {"E": 0, "O": 1}
BLOCKS = {"E": NX, "O": NZ}
Z_ORDER = (0, 4, 3, 5, 2, 6, 1, 7)


def group_rows(group):
    return sum(BLOCKS[kind] * ROWS for kind, _ in group)


def offset_of(g):
    return sum(group_rows(group) for group in GROUPS[:g]) // 2


FAR = (("p", 0), ("m", 1))
NEAR = (("p", 1), ("m", 0))
RING_ORDER = FAR + NEAR
FAR_LINKS = {"E": 2, "O": 1}


def hops_of(n, direction, half):
    return n // 2 if (direction, half) in FAR else n // 2 - 1


def fold(wide):
    return jnp.concatenate([wide[:, :HALF], wide[:, HALF:]], axis=0)


def unfold(folded):
    return jnp.concatenate([folded[:ROWS], folded[ROWS:]], axis=1)


def kernel(
    q_hbm,
    k_hbm,
    v_hbm,
    nk_hbm,
    nv_hbm,
    len_ref,
    res_hbm,
    gain_hbm,
    wg_hbm,
    wd_hbm,
    out_ref,
    q_ref,
    nk_ref,
    nv_ref,
    res_ref,
    gain_ref,
    k_ref,
    v_ref,
    wg_ref,
    wd_ref,
    sq_ref,
    ysend,
    yrecv,
    stream_ref,
    x_ref,
    xu_ref,
    p_ref,
    s1_send,
    s1_recv,
    s2_own,
    s2_send,
    s2_recv,
    hid_ref,
    d_ref,
    re_ref,
    ro_ref,
    fe_ref,
    fo_ref,
    zsend,
    zrecv,
    load_sem,
    send_sem,
    recv_sem,
):
    z = lax.axis_index("req")
    head = lax.axis_index("head")
    ffn = lax.axis_index("ffn")
    yq, core = head // 2, head % 2
    yh, x = ffn // NX, ffn % NX

    def along_z(step):
        return {"req": (z + step) % NZ}

    def along_x(step):
        return {"ffn": yh * NX + (x + step) % NX}

    def along_y(step):
        return {"head": ((yq + step) % NY) * 2 + core}

    other_core = {"head": yq * 2 + 1 - core}
    other_half = {"ffn": (1 - yh) * NX + x}

    def same_rows(dh, dk):
        return {"ffn": ((yh + dh) % 2) * NX + x, "head": (head + dk) % 8}

    loads = []
    for i, (src, dst) in enumerate(
        (
            (q_hbm, q_ref),
            (nk_hbm, nk_ref),
            (k_hbm, k_ref),
            (v_hbm, v_ref),
            (nv_hbm, nv_ref),
            (res_hbm, res_ref),
            (gain_hbm, gain_ref),
            (wg_hbm, wg_ref),
            (wd_hbm, wd_ref),
        )
    ):
        copy = pltpu.make_async_copy(src, dst, load_sem.at[i])
        copy.start()
        loads.append(copy)

    peers = [same_rows(dh, dk) for dh in range(2) for dk in range(8) if dh or dk]
    peers += [along_x(k) for k in range(1, NX)]
    peers += [along_z(k) for k in range(1, NZ)]
    barrier = pltpu.get_barrier_semaphore()
    for peer in peers:
        pl.semaphore_signal(barrier, inc=1, device_id=peer, device_id_type=MESH)

    copies = []

    def send(src, dst, device):
        i = len(copies)
        copy = pltpu.make_async_remote_copy(
            src_ref=src,
            dst_ref=dst,
            send_sem=send_sem.at[i],
            recv_sem=recv_sem.at[i],
            device_id=device,
            device_id_type=MESH,
        )
        copy.start()
        copies.append(copy)
        return copy

    for i in (0, 1, 4, 5, 6):
        loads[i].wait()
    q = q_ref[...].astype(F32)
    q_all = jnp.concatenate([q[:, HD * j : HD * (j + 1)] for j in range(HEADS)], axis=0)
    request = lax.broadcasted_iota(jnp.int32, (HEADS * ROWS, 1), 0) % ROWS
    limit = jnp.zeros((HEADS * ROWS, 1), jnp.int32)
    for r in range(ROWS):
        limit = jnp.where(request == r, len_ref[r], limit)
    scale = HD ** (-0.5)
    new_key = jnp.concatenate([nk_ref[...].astype(F32)] * HEADS, axis=0)
    new_value = jnp.concatenate([nv_ref[...].astype(F32)] * HEADS, axis=0)
    self_score = jnp.sum(q_all * new_key, axis=1, keepdims=True) * scale
    loads[2].wait()
    scores = jnp.zeros((HEADS * ROWS, CACHE), F32)
    for r in range(ROWS):
        scores += lax.dot_general(
            jnp.where(request == r, q_all, 0.0).astype(BF16),
            k_ref[r],
            (((1,), (1,)), ((), ())),
            preferred_element_type=F32,
        )
    scores = scores * scale
    visible = lax.broadcasted_iota(jnp.int32, scores.shape, 1) < limit
    maximum = jnp.maximum(
        jnp.max(jnp.where(visible, scores, -1e30), axis=1, keepdims=True), self_score
    )
    raised = jnp.where(visible, jnp.exp(scores - maximum), 0.0)
    self_raised = jnp.exp(self_score - maximum)
    totals = jnp.sum(raised, axis=1, keepdims=True) + self_raised
    weights = raised / totals
    self_weight = (self_raised / totals).astype(BF16).astype(F32)
    loads[3].wait()
    blended = self_weight * new_value
    for r in range(ROWS):
        blended += jnp.dot(
            jnp.where(request == r, weights, 0.0).astype(BF16),
            v_ref[r],
            preferred_element_type=F32,
        )
    attended = jnp.concatenate(
        [blended[ROWS * j : ROWS * (j + 1)] for j in range(HEADS)], axis=1
    ).astype(BF16)
    stream = (res_ref[...].astype(F32) + attended.astype(F32)).astype(BF16).astype(F32)
    stream_ref[...] = stream
    squares = stream * stream
    part = squares[:, :HD]
    for j in range(1, HEADS):
        part += squares[:, HD * j : HD * (j + 1)]
    sq_ref[0, 0] = part
    ysend[...] = fold(stream).astype(BF16)

    pl.semaphore_wait(barrier, len(peers))

    def send_squares(dh):
        return [
            send(sq_ref.at[0, 0], sq_ref.at[dh, (8 - dk) % 8], same_rows(dh, dk))
            for dk in range(8)
            if dh or dk
        ]

    sq_own = send_squares(0)
    ycopy = send(ysend, yrecv, other_half)
    sq_other = send_squares(1)
    gain = gain_ref[...].astype(F32).reshape(1, WIDTH)

    def normed(rows, dh):
        total = sq_ref[dh, 0]
        for dk in range(1, 8):
            total += sq_ref[dh, dk]
        inverse = lax.rsqrt(jnp.sum(total, axis=1, keepdims=True) / D + EPSILON)
        return fold(rows * inverse * gain).astype(BF16)

    o_first, e_first = {}, {}

    def first_sends(kind):
        if kind == "O":
            for copy in sq_own:
                copy.wait_recv()
            x_ref[1, 0] = normed(stream_ref[...], 0)
            for slot in range(1, NZ):
                o_first[slot] = send(
                    x_ref.at[1, 0], x_ref.at[1, slot], along_z(-Z_ORDER[slot])
                )
        else:
            for copy in sq_other:
                copy.wait_recv()
            ycopy.wait_recv()
            x_ref[0, 0] = normed(unfold(yrecv[...].astype(F32)), 1)
            for slot in (1, 2, 3):
                e_first[slot] = send(x_ref.at[0, 0], x_ref.at[0, slot], along_x(-slot))

    def first_end(kind, half):
        blocks = BLOCKS[kind] // 2
        for slot in range(half * blocks, (half + 1) * blocks):
            if slot:
                (e_first if kind == "E" else o_first)[slot].wait_recv()

    rings = {"E": (NZ, along_z), "O": (NX, along_x)}

    def chunk(ref, kind, slot, half):
        blocks = BLOCKS[kind] // 2
        return ref.at[FLOW[kind], pl.ds(slot * BLOCKS[kind] + half * blocks, blocks)]

    arriving, skipping = {}, {}

    def gather_end():
        for copy in skipping.values():
            copy.wait_recv()

    def gather_hop(kind, s, which=RING_ORDER):
        n, along = rings[kind]
        for direction, half in which:
            if (kind, direction, half, s - 1) in arriving:
                arriving[kind, direction, half, s - 1].wait_recv()
            step = 1 if direction == "p" else -1
            hops = hops_of(n, direction, half)
            skip = kind == "E" and hops == n // 2
            if s < hops - skip:
                arriving[kind, direction, half, s] = send(
                    chunk(x_ref, kind, (-step * s) % n, half),
                    chunk(x_ref, kind, (-step * (s + 1)) % n, half),
                    along(step),
                )
            if skip and s == hops - 2:
                skipping[direction] = send(
                    chunk(x_ref, kind, (-step * s) % n, half),
                    chunk(x_ref, kind, (-step * (s + 2)) % n, half),
                    along(2 * step),
                )

    step_copies = {}

    def gate(g):
        row = 0
        for kind, slot in GROUPS[g]:
            n = BLOCKS[kind]
            folded = x_ref[FLOW[kind], slot * n : (slot + 1) * n].astype(F32)
            low = folded[:, :ROWS].reshape(n * ROWS, HALF).astype(BF16)
            high = folded[:, ROWS:].reshape(n * ROWS, HALF).astype(BF16)
            xu_ref[row : row + n * ROWS, :HALF] = low
            xu_ref[row : row + n * ROWS, HALF:] = high
            row += n * ROWS
        m, o = row // 2, offset_of(g)
        value = jnp.dot(xu_ref[:row, :], wg_ref[...], preferred_element_type=F32)
        p_ref[0, o : o + m] = value[:m]
        p_ref[1, o : o + m] = value[m:]
        s1_send[o : o + m] = p_ref[1 - core, o : o + m].astype(BF16)
        step_copies[1, g] = [
            send(s1_send.at[pl.ds(o, m)], s1_recv.at[pl.ds(o, m)], other_core)
        ]

    def reduce_y(g):
        m, o = group_rows(GROUPS[g]) // 2, offset_of(g)
        for copy in step_copies[1, g]:
            copy.wait_recv()
        value = p_ref[core, o : o + m] + s1_recv[o : o + m].astype(F32)
        for j in range(NY):
            piece = value[:, QUARTER * j : QUARTER * (j + 1)]
            s2_own[j, o : o + m] = piece
            s2_send[j, o : o + m] = piece.astype(BF16)
        step_copies[2, g] = [
            send(
                s2_send.at[(yq + k) % NY, pl.ds(o, m)],
                s2_recv.at[k - 1, pl.ds(o, m)],
                along_y(k),
            )
            for k in (2, 1, 3)
        ]

    def activate(g):
        m, o = group_rows(GROUPS[g]) // 2, offset_of(g)
        for copy in step_copies[2, g]:
            copy.wait_recv()
        value = s2_own[yq, o : o + m]
        for k in range(NY - 1):
            value += s2_recv[k, o : o + m].astype(F32)
        hid_ref[core, yq, o : o + m] = (value / (1.0 + jnp.exp(-value))).astype(BF16)
        piece = hid_ref.at[core, yq, pl.ds(o, m)]
        step_copies[3, g] = [send(piece, piece, along_y(k)) for k in (2, 1, 3)]

    def share_core(g):
        m, o = group_rows(GROUPS[g]) // 2, offset_of(g)
        for copy in step_copies[3, g]:
            copy.wait_recv()
        piece = hid_ref.at[core, :, pl.ds(o, m)]
        step_copies[4, g] = [send(piece, piece, other_core)]

    def down(g):
        m, o = group_rows(GROUPS[g]) // 2, offset_of(g)
        for copy in step_copies[4, g]:
            copy.wait_recv()
        hidden = jnp.concatenate(
            [
                jnp.concatenate([hid_ref[c, j, o : o + m] for j in range(NY)], axis=1)
                for c in range(2)
            ],
            axis=0,
        )
        tile = 256
        for t in range(HALF // tile):
            columns = pl.ds(t * tile, tile)
            low = jnp.dot(
                hidden, wd_ref[:, t * tile : (t + 1) * tile], preferred_element_type=F32
            ).reshape(2 * m // ROWS, ROWS, tile)
            high = jnp.dot(
                hidden,
                wd_ref[:, HALF + t * tile : HALF + (t + 1) * tile],
                preferred_element_type=F32,
            ).reshape(2 * m // ROWS, ROWS, tile)
            both = jnp.concatenate([low, high], axis=1).astype(BF16)
            row = 0
            for kind, slot in GROUPS[g]:
                n = BLOCKS[kind]
                d_ref[FLOW[kind], slot * n : (slot + 1) * n, :, columns] = both[row : row + n]
                row += n

    recv_at = {"E": {}, "O": {}}
    for kind in ("E", "O"):
        n, _ = rings[kind]
        count = 0
        for direction, half in RING_ORDER:
            for s in range(hops_of(n, direction, half)):
                recv_at[kind][direction, half, s] = count
                count += 1
    recv_refs = {"E": re_ref, "O": ro_ref}
    sums = {}

    def scatter_hop(kind, s, which=RING_ORDER):
        n, along = rings[kind]
        landing = recv_refs[kind]
        blocks = BLOCKS[kind] // 2
        for direction, half in which:
            hops = hops_of(n, direction, half)
            step = 1 if direction == "p" else -1
            slot = (step * (hops - s)) % n
            links = FAR_LINKS[kind] if hops == n // 2 else 1
            joined = {e: [e - 1] for e in range(1 if links == 1 else 2, hops + 1)}
            if links > 1:
                joined[links] = [0] + joined[links]
            first = slot * BLOCKS[kind] + half * blocks
            if s in joined:
                value = d_ref[FLOW[kind], first : first + blocks].astype(F32)
                for t in joined[s]:
                    sums[kind, direction, half, t].wait_recv()
                    value += landing[recv_at[kind][direction, half, t]].astype(F32)
                d_ref[FLOW[kind], first : first + blocks] = value.astype(BF16)
            sums[kind, direction, half, s] = send(
                chunk(d_ref, kind, slot, half),
                landing.at[recv_at[kind][direction, half, s]],
                along(links * step if s == 0 else step),
            )

    def scatter_end(kind, half):
        n, _ = rings[kind]
        blocks = BLOCKS[kind] // 2
        value = d_ref[FLOW[kind], half * blocks : (half + 1) * blocks].astype(F32)
        for direction in ("p", "m"):
            hops = hops_of(n, direction, half)
            direct = [0] if hops == n // 2 == FAR_LINKS[kind] > 1 else []
            for t in direct + [hops - 1]:
                sums[kind, direction, half, t].wait_recv()
                value += recv_refs[kind][recv_at[kind][direction, half, t]].astype(F32)
        d_ref[FLOW[kind], half * blocks : (half + 1) * blocks] = value.astype(BF16)
        for slot in range(half * blocks, (half + 1) * blocks):
            if slot == 0:
                continue
            if kind == "O":
                last_copies[kind].append(
                    send(d_ref.at[1, slot], fo_ref.at[slot - 1], along_z(Z_ORDER[slot]))
                )
            else:
                last_copies[kind].append(
                    send(d_ref.at[0, slot], fe_ref.at[slot - 1], along_x(slot))
                )

    last_copies = {"E": [], "O": []}

    def last_end(kind):
        landing = fe_ref if kind == "E" else fo_ref
        value = d_ref[FLOW[kind], 0].astype(F32)
        for copy in last_copies[kind]:
            copy.wait_recv()
        for k in range(BLOCKS[kind] - 1):
            value += landing[k].astype(F32)
        return value

    first_sends("O")
    first_sends("E")
    first_end("E", 0)
    gather_hop("E", 0, (("p", 0), ("m", 0)))
    first_end("E", 1)
    gather_hop("E", 0, (("m", 1), ("p", 1)))
    first_end("O", 0)
    gather_hop("O", 0, (("p", 0), ("m", 0)))
    first_end("O", 1)
    gather_hop("O", 0, (("m", 1), ("p", 1)))
    loads[7].wait()
    gather_hop("E", 1)
    gate(0)
    gate(1)
    reduce_y(0)
    reduce_y(1)
    gather_hop("E", 2)
    gather_hop("O", 1)
    gate(2)
    reduce_y(2)
    gather_hop("E", 3)
    gate(3)
    activate(0)
    activate(1)
    reduce_y(3)
    gather_end()
    gather_hop("O", 2)
    gate(4)
    loads[8].wait()
    reduce_y(4)
    activate(2)
    activate(3)
    share_core(0)
    share_core(1)
    down(0)
    down(1)
    activate(4)
    share_core(2)
    down(2)
    scatter_hop("O", 0, NEAR)
    share_core(3)
    down(3)
    scatter_hop("E", 1, FAR)
    scatter_hop("E", 0, NEAR)
    share_core(4)
    down(4)
    scatter_hop("O", 0, FAR)
    scatter_hop("E", 0, FAR)
    scatter_hop("E", 2, FAR)
    scatter_hop("E", 1, NEAR)
    scatter_hop("O", 1, FAR)
    scatter_hop("E", 3, FAR)
    scatter_hop("E", 2, NEAR)
    scatter_end("O", 0)
    scatter_end("O", 1)
    scatter_end("E", 0)
    scatter_end("E", 1)
    zsend[...] = last_end("E").astype(BF16)
    zcopy = send(zsend, zrecv, other_half)
    total = last_end("O")
    zcopy.wait_recv()
    total += zrecv[...].astype(F32)
    out_ref[...] = (stream_ref[...] + unfold(total)).astype(BF16)

    for copy in copies:
        copy.wait_send()


COPIES = 1 + 15 + 7 + 3 + 14 + 6 + 8 * len(GROUPS) + 14 + 6 + 7 + 3 + 1


def per_device(
    queries,
    key_cache,
    value_cache,
    new_key,
    new_value,
    lengths,
    residual,
    norm_gain,
    w_gate,
    w_down,
):
    vmem = pl.BlockSpec(memory_space=pltpu.VMEM)
    smem = pl.BlockSpec(memory_space=pltpu.SMEM)
    hbm = pl.BlockSpec(memory_space=pl.ANY)
    block = (2 * ROWS, HALF)
    most = max(group_rows(group) for group in GROUPS)
    return pl.pallas_call(
        kernel,
        out_shape=jax.ShapeDtypeStruct((ROWS, WIDTH), BF16),
        in_specs=[hbm, hbm, hbm, hbm, hbm, smem, hbm, hbm, hbm, hbm],
        out_specs=vmem,
        scratch_shapes=[
            pltpu.VMEM((ROWS, WIDTH), BF16),
            pltpu.VMEM((ROWS, HD), BF16),
            pltpu.VMEM((ROWS, HD), BF16),
            pltpu.VMEM((ROWS, WIDTH), BF16),
            pltpu.VMEM((WIDTH,), BF16),
            pltpu.VMEM((ROWS, CACHE, HD), BF16),
            pltpu.VMEM((ROWS, CACHE, HD), BF16),
            pltpu.VMEM((WIDTH, HIDDEN), BF16),
            pltpu.VMEM((HIDDEN, WIDTH), BF16),
            pltpu.VMEM((2, 8, ROWS, HD), F32),
            pltpu.VMEM(block, BF16),
            pltpu.VMEM(block, BF16),
            pltpu.VMEM((ROWS, WIDTH), F32),
            pltpu.VMEM((2, NZ * NX) + block, BF16),
            pltpu.VMEM((most, WIDTH), BF16),
            pltpu.VMEM((2, 256, HIDDEN), F32),
            pltpu.VMEM((256, HIDDEN), BF16),
            pltpu.VMEM((256, HIDDEN), BF16),
            pltpu.VMEM((NY, 256, QUARTER), F32),
            pltpu.VMEM((NY, 256, QUARTER), BF16),
            pltpu.VMEM((NY - 1, 256, QUARTER), BF16),
            pltpu.VMEM((2, NY, 256, QUARTER), BF16),
            pltpu.VMEM((2, NZ * NX) + block, BF16),
            pltpu.VMEM((14, NX // 2) + block, BF16),
            pltpu.VMEM((6, NZ // 2) + block, BF16),
            pltpu.VMEM((NX - 1,) + block, BF16),
            pltpu.VMEM((NZ - 1,) + block, BF16),
            pltpu.VMEM(block, BF16),
            pltpu.VMEM(block, BF16),
            pltpu.SemaphoreType.DMA((9,)),
            pltpu.SemaphoreType.DMA((COPIES,)),
            pltpu.SemaphoreType.DMA((COPIES,)),
        ],
        compiler_params=pltpu.CompilerParams(
            collective_id=0, has_side_effects=True, vmem_limit_bytes=60 * 1024 * 1024
        ),
        cost_estimate=pl.CostEstimate(
            flops=2 * 2 * 512 * WIDTH * HIDDEN, bytes_accessed=6 * 2**20, transcendentals=0
        ),
    )(
        queries,
        key_cache,
        value_cache,
        new_key,
        new_value,
        lengths,
        residual,
        norm_gain,
        w_gate,
        w_down,
    )


def solution(mesh):
    rows = ("req", "ffn")
    return jax.shard_map(
        per_device,
        mesh=mesh,
        in_specs=(
            P(rows, "head"),
            P(rows, None, "head"),
            P(rows, None, "head"),
            P(rows, "head"),
            P(rows, "head"),
            P(rows),
            P(rows, "head"),
            P("head"),
            P("head", rows),
            P(rows, "head"),
        ),
        out_specs=P(rows, "head"),
        check_vma=False,
    )
```
